32 devices in a mesh: row: 8 (over y, x, core), col: 4 (over z).
Axes of the slice: x: 2, y: 2, z: 4, core: 2. Of those that a mesh axis runs over, the one named last changes fastest.
Arguments:
- pattern_in: int32 [32, 8], replicated, may hold values from 0 to 31, as said below
- pattern_mid: int32 [32, 8], replicated, may hold values from 0 to 31, as said below
- pattern_out: int32 [32, 8], replicated, may hold values from 0 to 31, as said below
- density_blocks: float32 [4, 8, 2, 4, 256, 256], P(None, 'row', None, 'col'), as said below
Outputs:
- purified_blocks: float32 [4, 8, 2, 4, 256, 256], P(None, 'row', None, 'col')
The draws below stay inside these ranges and needn't reach their ends.
Inputs may be any that keep to these rules, and one draw needn't show every extreme that they name: `pattern_in`: slot l * 4 + c of block row I names a block column congruent to c modulo 4; no column stands twice in a row; slot I mod 4 of row I names I; J stands in row I exactly when I stands in row J. `pattern_mid`: as for pattern_in. `pattern_out`: as for pattern_in. `density_blocks`: the block of row J for column I is the transpose of the block of row I for column J.
All inputs are finite; a program needn't handle non-finite values.
Results may differ from the reference program's by a relative error of at most 0.0091.
Values may be sent and summed in bfloat16 or wider, within the bound.
A program may use at most 128 MiB of HBM per device.

```python
import jax
import jax.numpy as jnp
from jax import lax

BS = 256
BR = 4
LZ = 2
ITERS = 2
GRID_ROWS = 8
GRID_COLS = 4
NB = 32
NZ = 8
OCC = 4096


def make_pattern(seed_key):
    classes = NZ // LZ
    members = NB // classes
    row_ids = jnp.arange(NB, dtype=jnp.int32)[:, None, None]
    slot_ids = jnp.arange(LZ, dtype=jnp.int32)[None, :, None]
    target_class = jnp.arange(classes, dtype=jnp.int32)[None, None, :]
    residue = row_ids % classes
    offset_in = row_ids // classes

    def one_perm(pair_id):
        return jax.random.permutation(jax.random.fold_in(seed_key, pair_id), members).astype(jnp.int32)
    perms = jax.vmap(one_perm)(jnp.arange(classes * classes, dtype=jnp.int32)).reshape(classes, classes, members)
    inverse = jnp.argsort(perms, axis=-1).astype(jnp.int32)
    forward = perms[residue, target_class, (offset_in + slot_ids) % members]
    backward = (inverse[target_class, residue, offset_in] - slot_ids) % members
    position = inverse[residue, residue, offset_in]
    partner = perms[residue, residue, position ^ 1]
    same_class = jnp.where(slot_ids == 0, offset_in, partner)
    target_off = jnp.where(residue < target_class, forward, jnp.where(residue > target_class, backward, same_class))
    column = target_class + classes * target_off
    return column.reshape(NB, NZ).astype(jnp.int32)


def draw_pattern_in(key, part):
    return make_pattern(jax.random.fold_in(key, 101))


def draw_pattern_mid(key, part):
    return make_pattern(jax.random.fold_in(key, 102))


def draw_pattern_out(key, part):
    return make_pattern(jax.random.fold_in(key, 103))


def draw_density_blocks(key, part):
    listed = make_pattern(jax.random.fold_in(key, 101))
    classes = NZ // LZ
    grid_rows = NB // BR
    value_key = jax.random.fold_in(key, 7)
    scales = jnp.exp(jax.random.uniform(jax.random.fold_in(value_key, 1), (NB, BS), jnp.float32, jnp.log(0.8), jnp.log(1.25)))
    entry_base = jnp.exp(jax.random.uniform(jax.random.fold_in(value_key, 2), (NB, BS), jnp.float32, jnp.log(0.7), jnp.log(1.4)))
    row_factor = jnp.exp(jax.random.uniform(jax.random.fold_in(value_key, 3), (NB,), jnp.float32, jnp.log(0.6), jnp.log(1.67)))
    target = jax.random.uniform(jax.random.fold_in(value_key, 4), (), jnp.float32, 0.9, 0.95)
    noise_level = 0.6
    ramp = 3.0 - 2.0 * (jnp.arange(NB) % grid_rows).astype(jnp.float32) / max(grid_rows - 1, 1)
    weights = entry_base * (ramp * row_factor)[:, None]
    diag_vals = weights * (target * (NB * BS * 0.5) / jnp.sum(weights))
    sigma = noise_level / jnp.sqrt(jnp.float32(NZ * BS))
    row_grid = jnp.broadcast_to(jnp.arange(NB, dtype=jnp.int32)[:, None], (NB, NZ)).reshape(-1)
    col_grid = listed.reshape(-1)
    identity = jnp.eye(BS, dtype=jnp.float32)

    def one_block(row_id, col_id):
        low_id = jnp.minimum(row_id, col_id)
        high_id = jnp.maximum(row_id, col_id)
        noise = jax.random.normal(jax.random.fold_in(value_key, 10 + low_id * NB + high_id), (BS, BS), jnp.float32)
        noise = jnp.where(row_id > col_id, noise.T, noise)
        noise = jnp.where(row_id == col_id, (noise + noise.T) * 0.7071067811865476, noise)
        mixed = scales[row_id][:, None] * (sigma * noise) * scales[col_id][None, :]
        return mixed + jnp.where(row_id == col_id, identity * diag_vals[row_id][None, :], 0.0)
    blocks = jax.vmap(one_block)(row_grid, col_grid)
    return blocks.reshape(BR, grid_rows, LZ, classes, BS, BS).astype(jnp.float32)


def setup_inputs(seed: int = 0) -> dict:
    key_of = jax.random.split(jax.random.key(seed), 5)
    return {
        "pattern_in": draw_pattern_in(jax.random.fold_in(key_of[4], 71), 0),
        "pattern_mid": draw_pattern_mid(jax.random.fold_in(key_of[4], 71), 0),
        "pattern_out": draw_pattern_out(jax.random.fold_in(key_of[4], 71), 0),
        "density_blocks": draw_density_blocks(jax.random.fold_in(key_of[4], 71), 0),
    }


def row_product(panels, cur_list, next_list, row_id):
    inner = cur_list[row_id]
    inner_safe = jnp.maximum(inner, 0)
    targets = next_list[row_id]
    candidates = cur_list[inner_safe]
    matches = (candidates[None, :, :] == targets[:, None, None]) & (inner >= 0)[None, :, None] & (targets >= 0)[:, None, None]
    partner = jnp.einsum("okm,kmuv->okuv", matches.astype(jnp.float32), panels[inner_safe], precision=lax.Precision.HIGHEST)
    return jnp.einsum("kuv,okvw->ouw", panels[row_id], partner, precision=lax.Precision.HIGHEST)


def purify(values, cur_list, next_list):
    row_ids = jnp.arange(NB, dtype=jnp.int32)
    on_cur = cur_list == row_ids[:, None]
    trace_now = jnp.sum(jnp.where(on_cur, jnp.trace(values, axis1=2, axis2=3), 0.0))
    rounded = values.astype(jnp.bfloat16)
    rounded = lax.optimization_barrier(rounded)
    panels = rounded.astype(jnp.float32)
    product = lax.map(lambda row_id: row_product(panels, cur_list, next_list, row_id), row_ids)
    keep = (cur_list[:, None, :] == next_list[:, :, None]) & (next_list >= 0)[:, :, None]
    previous = jnp.einsum("iom,imuv->iouv", keep.astype(jnp.float32), values, precision=lax.Precision.HIGHEST)
    return jnp.where(trace_now > OCC, product, 2.0 * previous - product)


def reference(pattern_in, pattern_mid, pattern_out, density_blocks):
    all_lists = (pattern_in, pattern_mid, pattern_out)
    values = density_blocks.reshape(NB, NZ, BS, BS)
    for iteration in range(ITERS):
        values = purify(values, all_lists[iteration], all_lists[iteration + 1])
    return values.reshape(BR, GRID_ROWS, LZ, GRID_COLS, BS, BS)
```

```python
import functools

import jax
import jax.numpy as jnp
from jax import lax
from jax.experimental import pallas as pl
from jax.experimental.pallas import tpu as pltpu
from jax.sharding import PartitionSpec as P

MESH = pl.DeviceIdType.MESH


def replicate_kernel(
    row_slots, grid_rows, grid_cols, main_ref, extra_ref, stat_ref, units_ref, total_ref,
    stat_buf, stat_in, local_sem, send_z, send_x, send_y, send_s, recv, stat_send, stat_recv,
):
    r = lax.axis_index("row")
    z = lax.axis_index("col")
    core = r % 2
    xpos = (r // 2) % 2
    sib = r + 1 - 2 * core
    rx = r + 2 - 4 * xpos
    ry = (r + grid_rows // 2) % grid_rows
    rd = (rx + grid_rows // 2) % grid_rows
    peers = [z + 1 - 2 * (z % 2), (z + 2) % grid_cols, grid_cols - 1 - z]
    zdiag = r % grid_cols
    half = row_slots // 2
    base = grid_rows * grid_cols * row_slots
    extra_half = half // 2

    def span(row, chunk, h):
        if isinstance(chunk, str):
            return pl.ds(base + row * half + h * extra_half, extra_half)
        return pl.ds((row * grid_cols + chunk) * row_slots + h * half, half)

    def rsem(row, chunk, h):
        return recv.at[row, grid_cols if isinstance(chunk, str) else chunk, h]

    barrier = pltpu.get_barrier_semaphore()
    targets = [(sib, z), (rx, z), (ry, z)] + [(r, q) for q in peers]
    for target in targets:
        pl.semaphore_signal(barrier, inc=1, device_id=target, device_id_type=MESH)
    pl.semaphore_wait(barrier, len(targets))

    started = []

    def send(src, row, chunk, h, sem, target):
        copy = pltpu.make_async_remote_copy(
            src_ref=src,
            dst_ref=units_ref.at[span(row, chunk, h)],
            send_sem=sem,
            recv_sem=rsem(row, chunk, h),
            device_id=target,
            device_id_type=MESH,
        )
        copy.start()
        started.append(copy)

    def wait_in(row, chunk, h):
        ref = units_ref.at[span(row, chunk, h)]
        pltpu.make_async_remote_copy(
            src_ref=ref, dst_ref=ref, send_sem=local_sem.at[0], recv_sem=rsem(row, chunk, h),
            device_id=(sib, z), device_id_type=MESH,
        ).wait_recv()

    def mine(h):
        return main_ref.at[pl.ds(h * half, half)]

    def mine_extra(h):
        return extra_ref.at[pl.ds(h * extra_half, extra_half)]

    for h in range(2):
        for j in (2, 1, 0):
            send(mine(h), r, z, h, send_z.at[j, 0, h], (r, peers[j]))
        send(mine(h), r, z, h, send_x.at[0, h], (rx, z))
        send(mine(h), r, z, h, send_y.at[0, h], (ry, z))
        send(mine(h), r, z, h, send_s.at[0, 0, h], (sib, z))

    @pl.when(z == zdiag)
    def _():
        for h in range(2):
            for j in range(3):
                pltpu.make_async_remote_copy(
                    src_ref=mine_extra(h), dst_ref=units_ref.at[span(r, "e", h)],
                    send_sem=send_z.at[j, 1, h], recv_sem=rsem(r, "e", h),
                    device_id=(r, peers[j]), device_id_type=MESH,
                ).start()

    keep = pltpu.make_async_copy(
        main_ref, units_ref.at[pl.ds((r * grid_cols + z) * row_slots, row_slots)], local_sem.at[1]
    )
    keep.start()

    @pl.when(z == zdiag)
    def _():
        own = pltpu.make_async_copy(
            extra_ref, units_ref.at[pl.ds(base + r * half, half)], local_sem.at[2]
        )
        own.start()
        own.wait()

    stat_buf[0] = stat_ref[...]
    for j, target in enumerate(((sib, z), (rx, z), (ry, z))):
        copy = pltpu.make_async_remote_copy(
            src_ref=stat_buf.at[j], dst_ref=stat_in.at[j], send_sem=stat_send.at[j],
            recv_sem=stat_recv.at[j], device_id=target, device_id_type=MESH,
        )
        copy.start()
        copy.wait()
        stat_buf[j + 1] = stat_buf[j] + stat_in[j]
    stat_copies = []
    for j in range(3):
        copy = pltpu.make_async_remote_copy(
            src_ref=stat_buf.at[3], dst_ref=stat_in.at[3 + j], send_sem=stat_send.at[3 + j],
            recv_sem=stat_recv.at[3 + j], device_id=(r, peers[j]), device_id_type=MESH,
        )
        copy.start()
        stat_copies.append(copy)

    def from_plane(chunk, k):
        for h in range(2):
            wait_in(rx, chunk, h)
            src = units_ref.at[span(rx, chunk, h)]
            if h == 0:
                send(src, rx, chunk, h, send_y.at[grid_cols + 1 + k, 0], (ry, z))
            send(src, rx, chunk, h, send_s.at[1, k, h], (sib, z))
            wait_in(ry, chunk, h)
            src = units_ref.at[span(ry, chunk, h)]
            if h == 1:
                send(src, ry, chunk, h, send_x.at[grid_cols + 1 + k, 0], (rx, z))
            send(src, ry, chunk, h, send_s.at[2, k, h], (sib, z))

    def from_col(chunk, k):
        for h in range(2):
            if isinstance(chunk, str):
                @pl.when(z != zdiag)
                def _():
                    wait_in(r, chunk, h)
            else:
                wait_in(r, chunk, h)
            src = units_ref.at[span(r, chunk, h)]
            send(src, r, chunk, h, send_x.at[k, h], (rx, z))
            send(src, r, chunk, h, send_y.at[k, h], (ry, z))
            send(src, r, chunk, h, send_s.at[0, k, h], (sib, z))

    chunks = [z] + peers + ["e"]
    for k in range(1, len(chunks)):
        from_col(chunks[k], k)
        from_plane(chunks[k - 1], k - 1)
    from_plane(chunks[-1], len(chunks) - 1)

    for copy in stat_copies:
        copy.wait()
    near = stat_buf[3] + stat_in[3]
    far = stat_in[4] + stat_in[5]
    total_ref[...] = near + far

    for k, chunk in enumerate(chunks):
        for h in range(2):
            wait_in(rd, chunk, h)
            send(units_ref.at[span(rd, chunk, h)], rd, chunk, h, send_s.at[3, k, h], (sib, z))
    for row in (sib, sib + rx - r, (sib + grid_rows // 2) % grid_rows,
                (sib + rx - r + grid_rows // 2) % grid_rows):
        for chunk in chunks:
            for h in range(2):
                wait_in(row, chunk, h)
    for copy in started:
        copy.wait_send()

    @pl.when(z == zdiag)
    def _():
        for h in range(2):
            for j in range(3):
                pltpu.make_async_remote_copy(
                    src_ref=mine_extra(h), dst_ref=units_ref.at[span(r, "e", h)],
                    send_sem=send_z.at[j, 1, h], recv_sem=rsem(r, "e", h),
                    device_id=(r, peers[j]), device_id_type=MESH,
                ).wait_send()
    keep.wait()


def purify_kernel(
    grid_rows, grid_cols, info, l0, l1, l2, units_hbm, own_ref, out_ref,
    units, lhs, rhs, acc, cache, exact, done, sem,
):
    load = pltpu.make_async_copy(units_hbm, units, sem)
    load.start()
    r, c, up0, up1 = info[0], info[1], info[2], info[3]
    block_rows = out_ref.shape[0] // 2
    total_rows = grid_rows * block_rows
    slots = 2 * grid_cols
    row_slots = 2 * block_rows
    base = grid_rows * grid_cols * row_slots
    edge = out_ref.shape[1]
    mid = edge // 2

    def panel(i):
        return jnp.where(i % grid_cols == c, block_rows + i // grid_cols, i // grid_rows)

    def in_list(lists, i, j):
        cls = j % grid_cols
        first = lists[i, cls] == j
        second = lists[i, grid_cols + cls] == j
        return jnp.where(first, 0, jnp.where(second, 1, 2))

    def before(i, j):
        ci, cj = i % grid_cols, j % grid_cols
        return (ci < cj) | ((ci == cj) & (i < j))

    def unit_of(i, j):
        at = (i % grid_rows) * grid_cols + j % grid_cols
        return at * row_slots + (i // grid_rows) * 2 + jnp.minimum(in_list(l0, i, j), 1)

    def halves(i, j):
        swap = before(j, i)
        lo = jnp.where(swap, j, i)
        hi = jnp.where(swap, i, j)
        top = unit_of(lo, hi)
        diag = base + (i % grid_rows) * block_rows + i // grid_rows
        low = jnp.where(i == j, diag, unit_of(hi, lo))
        return swap, top, low

    def load_oriented(i, j):
        swap, top, low = halves(i, j)

        @pl.when(swap)
        def _():
            lhs[:, :mid] = units[top].T
            lhs[:, mid:] = units[low].T

        @pl.when(jnp.logical_not(swap))
        def _():
            lhs[:mid, :] = units[top]
            lhs[mid:, :] = units[low]

    def first_product(i, j):
        acc[...] = jnp.zeros_like(acc)

        @pl.loop(0, slots)
        def _(m):
            k = l0[i, m]

            @pl.when(in_list(l0, k, j) < 2)
            def _():
                load_oriented(i, k)
                swap, top, low = halves(k, j)
                rhs[:mid, :] = units[top]
                rhs[mid:, :] = units[low]

                @pl.when(swap)
                def _():
                    acc[...] += lax.dot_general(
                        lhs[...], rhs[...], (((1,), (1,)), ((), ())),
                        preferred_element_type=jnp.float32,
                    )

                @pl.when(jnp.logical_not(swap))
                def _():
                    acc[...] += jnp.dot(lhs[...], rhs[...], preferred_element_type=jnp.float32)

    @pl.loop(0, 3 * block_rows)
    def _(p):
        for k in range(slots):
            done[p, k] = 0

    load.wait()

    @pl.loop(0, 2 * block_rows)
    def _(o):
        i = (o // 2) * grid_rows + r
        slot = (o % 2) * grid_cols + c
        j = l1[i, slot]
        first_product(i, j)

        @pl.when(up0 == 0)
        def _():
            at = in_list(l0, i, j)

            @pl.when(at < 2)
            def _():
                acc[...] = 2.0 * own_ref[(o // 2) * 2 + jnp.minimum(at, 1)] - acc[...]

            @pl.when(at == 2)
            def _():
                acc[...] = -acc[...]

        exact[o] = acc[...]
        cache[panel(i), slot] = acc[...].astype(jnp.bfloat16)
        done[panel(i), slot] = 1

    def ensure(i, slot):
        @pl.when(done[panel(i), slot] == 0)
        def _():
            j = l1[i, slot]
            first_product(i, j)

            @pl.when(up0 == 0)
            def _():
                at = in_list(l0, i, j)

                @pl.when(at < 2)
                def _():
                    load_oriented(i, j)
                    acc[...] = 2.0 * lhs[...].astype(jnp.float32) - acc[...]

                @pl.when(at == 2)
                def _():
                    acc[...] = -acc[...]

            cache[panel(i), slot] = acc[...].astype(jnp.bfloat16)
            done[panel(i), slot] = 1

    @pl.loop(0, 2 * block_rows)
    def _(o):
        i = (o // 2) * grid_rows + r
        j = l2[i, (o % 2) * grid_cols + c]
        out_ref[o] = jnp.zeros(out_ref.shape[1:], jnp.float32)

        @pl.loop(0, slots)
        def _(m):
            k = l1[i, m]
            at = in_list(l1, j, k)

            @pl.when(at < 2)
            def _():
                other = jnp.minimum(at, 1) * grid_cols + k % grid_cols

                @pl.loop(0, 2)
                def _(side):
                    ensure(jnp.where(side == 0, i, j), jnp.where(side == 0, m, other))

                out_ref[o] += lax.dot_general(
                    cache[panel(i), m], cache[panel(j), other], (((1,), (1,)), ((), ())),
                    preferred_element_type=jnp.float32,
                )

        @pl.when(up1 == 0)
        def _():
            at = in_list(l1, i, j)

            @pl.when(at < 2)
            def _():
                out_ref[o] = 2.0 * exact[(o // 2) * 2 + jnp.minimum(at, 1)] - out_ref[o]

            @pl.when(at == 2)
            def _():
                out_ref[o] = -out_ref[o]


def replicated(pattern_in, pattern_mid, pattern_out, density):
    grid_rows = lax.axis_size("row")
    grid_cols = lax.axis_size("col")
    r = lax.axis_index("row")
    c = lax.axis_index("col")
    block_rows, _, pairs, _, edge, _ = density.shape
    mid = edge // 2
    row_slots = block_rows * pairs
    total_rows = grid_rows * block_rows
    occupied = total_rows * edge / 2.0
    owned = density.reshape(block_rows, pairs, edge, edge)
    rounded = owned.astype(jnp.bfloat16)

    cls = r % grid_cols
    own_index = jnp.arange(block_rows, dtype=jnp.int32) * grid_rows + r
    partner = pattern_in[own_index, grid_cols + c]
    first = jnp.where(
        cls == c,
        jnp.stack([jnp.ones((block_rows,), bool), own_index < partner], axis=1),
        cls < c,
    )
    top = rounded[:, :, :mid, :]
    low = jnp.swapaxes(rounded[:, :, :, mid:], 2, 3)
    main = jnp.where(first[..., None, None], top, low).reshape(row_slots, mid, edge)
    extra = rounded[:, 0, mid:, :]

    diag = jnp.sum(jnp.where(jnp.eye(edge, dtype=bool), owned[:, 0], 0.0))
    trace_part = jnp.where(cls == c, diag, 0.0)
    square_part = jnp.sum(jnp.square(rounded.astype(jnp.float32)))
    stat = jnp.where(jnp.arange(8)[:, None] < 4, trace_part, square_part) * jnp.ones((8, 128), jnp.float32)

    units = grid_rows * grid_cols * row_slots + total_rows
    chunks = grid_cols + 1
    dma = pltpu.SemaphoreType.DMA
    everything, total = pl.pallas_call(
        functools.partial(replicate_kernel, row_slots, grid_rows, grid_cols),
        out_shape=(
            jax.ShapeDtypeStruct((units, mid, edge), jnp.bfloat16),
            jax.ShapeDtypeStruct((8, 128), jnp.float32),
        ),
        in_specs=[
            pl.BlockSpec(memory_space=pl.ANY),
            pl.BlockSpec(memory_space=pl.ANY),
            pl.BlockSpec(memory_space=pltpu.VMEM),
        ],
        out_specs=(pl.BlockSpec(memory_space=pl.ANY), pl.BlockSpec(memory_space=pltpu.VMEM)),
        scratch_shapes=[
            pltpu.VMEM((4, 8, 128), jnp.float32),
            pltpu.VMEM((6, 8, 128), jnp.float32),
            dma((3,)),
            dma((3, 2, 2)),
            dma((2 * chunks, 2)),
            dma((2 * chunks, 2)),
            dma((4, chunks, 2)),
            dma((grid_rows, chunks, 2)),
            dma((6,)),
            dma((6,)),
        ],
        compiler_params=pltpu.CompilerParams(collective_id=0, has_side_effects=True),
    )(main, extra, stat)

    trace0 = total[0, 0]
    squares = total[4, 0]
    up0 = trace0 > occupied
    trace1 = jnp.where(up0, squares, 2.0 * trace0 - squares)
    up1 = trace1 > occupied
    info = jnp.stack([r, c, up0.astype(jnp.int32), up1.astype(jnp.int32)]).astype(jnp.int32)

    smem = pl.BlockSpec(memory_space=pltpu.SMEM)
    out = pl.pallas_call(
        functools.partial(purify_kernel, grid_rows, grid_cols),
        out_shape=jax.ShapeDtypeStruct((row_slots, edge, edge), jnp.float32),
        in_specs=[smem] * 4 + [
            pl.BlockSpec(memory_space=pl.ANY),
            pl.BlockSpec(memory_space=pltpu.VMEM),
        ],
        out_specs=pl.BlockSpec(memory_space=pltpu.VMEM),
        scratch_shapes=[
            pltpu.VMEM((units, mid, edge), jnp.bfloat16),
            pltpu.VMEM((edge, edge), jnp.bfloat16),
            pltpu.VMEM((edge, edge), jnp.bfloat16),
            pltpu.VMEM((edge, edge), jnp.float32),
            pltpu.VMEM((3 * block_rows, 2 * grid_cols, edge, edge), jnp.bfloat16),
            pltpu.VMEM((row_slots, edge, edge), jnp.float32),
            pltpu.SMEM((3 * block_rows, 2 * grid_cols), jnp.int32),
            pltpu.SemaphoreType.DMA,
        ],
        compiler_params=pltpu.CompilerParams(vmem_limit_bytes=56 * 1024 * 1024),
    )(info, pattern_in, pattern_mid, pattern_out, everything, owned.reshape(row_slots, edge, edge))
    return out.reshape(density.shape)


ITERS = 2


def purify_section(owned, cur_list, next_list, grid_rows, grid_cols, row_index, col_index):
    block_rows = owned.shape[0]
    slot_pairs = owned.shape[2]
    edge_size = owned.shape[4]
    total_rows = cur_list.shape[0]
    slot_count = cur_list.shape[1]
    occupied = total_rows * edge_size / 2.0
    panels = owned.astype(jnp.bfloat16)
    owned_slots = owned[:, 0, :, 0]
    my_rows = lax.dynamic_index_in_dim(
        cur_list.reshape(block_rows, grid_rows, slot_count), row_index, axis=1, keepdims=False
    )
    my_residue = lax.dynamic_index_in_dim(
        my_rows.reshape(block_rows, slot_pairs, grid_cols), col_index, axis=2, keepdims=False
    )
    own_index = jnp.arange(block_rows, dtype=jnp.int32) * grid_rows + row_index
    diag_term = jnp.sum(
        jnp.where(my_residue == own_index[:, None], jnp.trace(owned_slots, axis1=2, axis2=3), 0.0)
    )
    next_trace = None
    trace_now = lax.psum(diag_term, ("row", "col"))
    gathered_rows = lax.all_gather(panels, "col", axis=3, tiled=True).reshape(
        block_rows, slot_count, edge_size, edge_size
    )
    next_rows = lax.dynamic_index_in_dim(
        next_list.reshape(block_rows, grid_rows, slot_count), row_index, axis=1, keepdims=False
    )
    out_cols = lax.dynamic_index_in_dim(
        next_rows.reshape(block_rows, slot_pairs, grid_cols), col_index, axis=2, keepdims=False
    )
    inner_safe = jnp.maximum(my_rows, 0)
    valid_inner = my_rows >= 0
    valid_out = out_cols >= 0
    column_panels = lax.all_gather(panels, "row", axis=1, tiled=True).reshape(
        total_rows * slot_pairs, edge_size, edge_size
    )
    residue_lists = lax.dynamic_index_in_dim(
        cur_list.reshape(total_rows, slot_pairs, grid_cols), col_index, axis=2, keepdims=False
    )
    candidates = residue_lists[inner_safe]
    matches = (
        (candidates[:, None, :, :] == out_cols[:, :, None, None])
        & valid_inner[:, None, :, None]
        & valid_out[:, :, None, None]
    )
    chosen = jnp.sum(matches * jnp.arange(slot_pairs, dtype=jnp.int32), axis=-1)
    present = jnp.any(matches, axis=-1)
    position = inner_safe[:, None, :] * slot_pairs + chosen
    picked = jnp.where(
        present[..., None, None], column_panels[position], jnp.zeros((), jnp.bfloat16)
    )
    product = jnp.einsum(
        "ikuv,ilkvw->iluw", gathered_rows, picked, preferred_element_type=jnp.float32
    )
    keep = (my_residue[:, None, :] == out_cols[:, :, None]) & valid_out[:, :, None]
    previous = jnp.sum(jnp.where(keep[..., None, None], owned_slots[:, None], 0.0), axis=2)
    updated = jnp.where(trace_now > occupied, product, 2.0 * previous - product)
    return (updated.reshape(block_rows, 1, slot_pairs, 1, edge_size, edge_size), next_trace)


def shards(pattern_in, pattern_mid, pattern_out, density_blocks):
    grid_rows = lax.axis_size("row")
    grid_cols = lax.axis_size("col")
    row_index = lax.axis_index("row")
    col_index = lax.axis_index("col")
    all_lists = (pattern_in, pattern_mid, pattern_out)
    current = density_blocks
    for iteration in range(ITERS):
        current, known_trace = purify_section(
            current,
            all_lists[iteration],
            all_lists[iteration + 1],
            grid_rows,
            grid_cols,
            row_index,
            col_index,
        )
    return current


def solution(mesh):
    in_specs = (P(), P(), P(), P(None, "row", None, "col", None, None))
    out_specs = P(None, "row", None, "col", None, None)
    plane = mesh.shape["row"] == 2 * 2 * 2 and mesh.shape["col"] == 2 * 2
    body = replicated if plane else shards
    return jax.shard_map(body, mesh=mesh, in_specs=in_specs, out_specs=out_specs, check_vma=False)
```

```python
import functools

import jax
import jax.numpy as jnp
from jax import lax
from jax.experimental import pallas as pl
from jax.experimental.pallas import tpu as pltpu
from jax.sharding import PartitionSpec as P

MESH = pl.DeviceIdType.MESH


def replicate_kernel(
    grid_rows, grid_cols, own_ref, list_ref, units_ref, total_ref,
    main_ref, extra_ref, stat_buf, stat_in,
    local_sem, send_z, send_x, send_y, send_s, recv, stat_send, stat_recv,
):
    r = lax.axis_index("row")
    z = lax.axis_index("col")
    row_slots, mid, edge = main_ref.shape
    core = r % 2
    xpos = (r // 2) % 2
    sib = r + 1 - 2 * core
    rx = r + 2 - 4 * xpos
    ry = (r + grid_rows // 2) % grid_rows
    rd = (rx + grid_rows // 2) % grid_rows
    last = grid_cols - 1
    side = z // 2
    peers = [z + 1 - 2 * (z % 2), 2 - side, last - last * side]
    pairwise = [z + 1 - 2 * (z % 2), (z + 2) % grid_cols, last - z]
    zdiag = r % grid_cols
    half = row_slots // 2
    base = grid_rows * grid_cols * row_slots
    extra_half = half // 2

    def span(row, chunk, h):
        if isinstance(chunk, str):
            return pl.ds(base + row * half + h * extra_half, extra_half)
        return pl.ds((row * grid_cols + chunk) * row_slots + h * half, half)

    def rsem(row, chunk, h):
        return recv.at[row, grid_cols if isinstance(chunk, str) else chunk, h]

    barrier = pltpu.get_barrier_semaphore()
    targets = [(sib, z), (rx, z), (ry, z)] + [(r, q) for q in peers]
    for target in targets:
        pl.semaphore_signal(barrier, inc=1, device_id=target, device_id_type=MESH)

    def pack(o):
        @pl.when(zdiag < z)
        def _():
            main_ref[o] = own_ref[o, :mid, :].astype(jnp.bfloat16)

        @pl.when(zdiag > z)
        def _():
            main_ref[o] = own_ref[o, :, mid:].astype(jnp.bfloat16).T

        @pl.when(zdiag == z)
        def _():
            top = own_ref[o, :mid, :].astype(jnp.bfloat16)
            if o % 2 == 0:
                main_ref[o] = top
                extra_ref[o // 2] = own_ref[o, mid:, :].astype(jnp.bfloat16)
            else:
                index = (o // 2) * grid_rows + r
                low = own_ref[o, :, mid:].astype(jnp.bfloat16).T
                main_ref[o] = jnp.where(index < list_ref[index, grid_cols + z], top, low)

    pending = []

    def send(src, row, chunk, h, sem, target, cond=None):
        copy = pltpu.make_async_remote_copy(
            src_ref=src,
            dst_ref=units_ref.at[span(row, chunk, h)],
            send_sem=sem,
            recv_sem=rsem(row, chunk, h),
            device_id=target,
            device_id_type=MESH,
        )
        if cond is None:
            copy.start()
        else:
            pl.when(cond)(copy.start)
        pending.append((cond, copy))

    def wait_in(row, chunk, h):
        ref = units_ref.at[span(row, chunk, h)]
        pltpu.make_async_remote_copy(
            src_ref=ref, dst_ref=ref, send_sem=local_sem.at[0], recv_sem=rsem(row, chunk, h),
            device_id=(sib, z), device_id_type=MESH,
        ).wait_recv()

    def send_col(src, chunk, origin, k, h):
        send(src, r, chunk, h, send_z.at[0, k, h], (r, (z + 1) % grid_cols), (origin <= z) & (z < last))
        send(src, r, chunk, h, send_z.at[1, k, h], (r, (z + last) % grid_cols), (origin >= z) & (z > 0))

    for h in range(2):
        for o in range(h * half, (h + 1) * half):
            pack(o)
        if h == 0:
            pl.semaphore_wait(barrier, len(targets))
        src = main_ref.at[pl.ds(h * half, half)]
        send_col(src, z, z, 0, h)
        send(src, r, z, h, send_x.at[0, h], (rx, z))
        send(src, r, z, h, send_y.at[0, h], (ry, z))
        send(src, r, z, h, send_s.at[0, 0, h], (sib, z))

    keep = pltpu.make_async_copy(
        main_ref, units_ref.at[pl.ds((r * grid_cols + z) * row_slots, row_slots)], local_sem.at[1]
    )
    keep.start()

    @pl.when(z == zdiag)
    def _():
        own = pltpu.make_async_copy(
            extra_ref, units_ref.at[pl.ds(base + r * half, half)], local_sem.at[2]
        )
        own.start()
        own.wait()

    def lanes(v):
        v = jnp.sum(v.reshape(edge // 8, 8, edge), axis=0)
        out = v[:, :128]
        for at in range(128, edge, 128):
            out = out + v[:, at:at + 128]
        return out

    stat_buf[0] = jnp.zeros(stat_buf.shape[1:], jnp.float32)
    for o in range(row_slots):
        stat_buf[0, 1] += lanes(jnp.square(own_ref[o].astype(jnp.bfloat16).astype(jnp.float32)))

    @pl.when(z == zdiag)
    def _():
        rows = lax.broadcasted_iota(jnp.int32, (edge, edge), 0)
        cols = lax.broadcasted_iota(jnp.int32, (edge, edge), 1)
        for o in range(0, row_slots, 2):
            stat_buf[0, 0] += lanes(jnp.where(rows == cols, own_ref[o], 0.0))

    plane = ((sib, z), (rx, z), (ry, z))

    def stat_copy(slot, src, target):
        return pltpu.make_async_remote_copy(
            src_ref=stat_buf.at[src], dst_ref=stat_in.at[slot], send_sem=stat_send.at[slot],
            recv_sem=stat_recv.at[slot], device_id=target, device_id_type=MESH,
        )

    def stat_step(j):
        if 0 < j <= 3:
            stat_copy(j - 1, j - 1, plane[j - 1]).wait()
            stat_buf[j] = stat_buf[j - 1] + stat_in[j - 1]
        if j < 3:
            stat_copy(j, j, plane[j]).start()
        if j == 3:
            for k in range(3):
                stat_copy(3 + k, 3, (r, pairwise[k])).start()

    def from_plane(chunk, k):
        for h in range(2):
            wait_in(rx, chunk, h)
            src = units_ref.at[span(rx, chunk, h)]
            if h == 0:
                send(src, rx, chunk, h, send_y.at[grid_cols + 1 + k, 0], (ry, z))
            send(src, rx, chunk, h, send_s.at[1, k, h], (sib, z))
            wait_in(ry, chunk, h)
            src = units_ref.at[span(ry, chunk, h)]
            if h == 1:
                send(src, ry, chunk, h, send_x.at[grid_cols + 1 + k, 0], (rx, z))
            send(src, ry, chunk, h, send_s.at[2, k, h], (sib, z))

    def from_col(chunk, k):
        for h in range(2):
            if isinstance(chunk, str):
                @pl.when(z != zdiag)
                def _():
                    wait_in(r, chunk, h)
            else:
                wait_in(r, chunk, h)
            src = units_ref.at[span(r, chunk, h)]
            send_col(src, chunk, zdiag if isinstance(chunk, str) else chunk, k, h)
            send(src, r, chunk, h, send_x.at[k, h], (rx, z))
            send(src, r, chunk, h, send_y.at[k, h], (ry, z))
            send(src, r, chunk, h, send_s.at[0, k, h], (sib, z))

    chunks = [z] + peers + ["e"]
    stat_step(0)
    for k in range(1, len(chunks)):
        from_col(chunks[k], k)
        stat_step(k)
        from_plane(chunks[k - 1], k - 1)
    from_plane(chunks[-1], len(chunks) - 1)

    for k in range(3):
        stat_copy(3 + k, 3, (r, pairwise[k])).wait()
    near = stat_buf[3] + stat_in[3]
    total_ref[...] = near + (stat_in[4] + stat_in[5])

    for k, chunk in enumerate(chunks):
        for h in range(2):
            wait_in(rd, chunk, h)
            send(units_ref.at[span(rd, chunk, h)], rd, chunk, h, send_s.at[3, k, h], (sib, z))
    for row in (sib, sib + rx - r, (sib + grid_rows // 2) % grid_rows,
                (sib + rx - r + grid_rows // 2) % grid_rows):
        for chunk in chunks:
            for h in range(2):
                wait_in(row, chunk, h)
    for cond, copy in pending:
        if cond is None:
            copy.wait_send()
        else:
            pl.when(cond)(copy.wait_send)
    keep.wait()


def purify_kernel(
    grid_rows, grid_cols, l0, l1, l2, total_ref, units_hbm, own_ref, out_ref,
    units, lhs, acc, cache, exact, done, sem,
):
    load = pltpu.make_async_copy(units_hbm, units, sem)
    load.start()
    r = lax.axis_index("row")
    c = lax.axis_index("col")
    block_rows = out_ref.shape[0] // 2
    total_rows = grid_rows * block_rows
    slots = 2 * grid_cols
    row_slots = 2 * block_rows
    base = grid_rows * grid_cols * row_slots
    edge = out_ref.shape[1]
    mid = edge // 2
    occupied = total_rows * edge / 2.0
    trace0 = jnp.sum(total_ref[0])
    squares = jnp.sum(total_ref[1])
    up0 = (trace0 > occupied).astype(jnp.int32)
    up1 = (jnp.where(up0 == 1, squares, 2.0 * trace0 - squares) > occupied).astype(jnp.int32)

    def col_of(i):
        return lax.rem(i, jnp.int32(grid_cols)) if grid_cols & (grid_cols - 1) else i & (grid_cols - 1)

    def row_of(i):
        return lax.rem(i, jnp.int32(grid_rows)) if grid_rows & (grid_rows - 1) else i & (grid_rows - 1)

    def by_row(i):
        return lax.div(i, jnp.int32(grid_rows)) if grid_rows & (grid_rows - 1) else i >> (grid_rows.bit_length() - 1)

    def by_col(i):
        return lax.div(i, jnp.int32(grid_cols)) if grid_cols & (grid_cols - 1) else i >> (grid_cols.bit_length() - 1)

    def panel(i):
        return jnp.where(col_of(i) == c, block_rows + by_col(i), by_row(i))

    def in_list(lists, i, j):
        cls = col_of(j)
        first = lists[i, cls] == j
        second = lists[i, grid_cols + cls] == j
        return jnp.where(first, 0, jnp.where(second, 1, 2))

    def before(i, j):
        ci, cj = col_of(i), col_of(j)
        return (ci < cj) | ((ci == cj) & (i < j))

    def unit_of(i, j):
        at = (row_of(i)) * grid_cols + col_of(j)
        return at * row_slots + (by_row(i)) * 2 + jnp.minimum(in_list(l0, i, j), 1)

    def halves(i, j):
        swap = before(j, i)
        lo = jnp.where(swap, j, i)
        hi = jnp.where(swap, i, j)
        top = unit_of(lo, hi)
        diag = base + (row_of(i)) * block_rows + by_row(i)
        low = jnp.where(i == j, diag, unit_of(hi, lo))
        return swap, top, low

    def load_oriented(i, j):
        swap, top, low = halves(i, j)

        @pl.when(swap)
        def _():
            lhs[:, :mid] = units[top].T
            lhs[:, mid:] = units[low].T

        @pl.when(jnp.logical_not(swap))
        def _():
            lhs[:mid, :] = units[top]
            lhs[mid:, :] = units[low]

    def first_product(i, j):
        acc[...] = jnp.zeros_like(acc)

        @pl.loop(0, slots)
        def _(m):
            k = l0[i, m]

            @pl.when(in_list(l0, k, j) < 2)
            def _():
                swap_l, top_l, low_l = halves(i, k)
                swap_r, top_r, low_r = halves(k, j)
                for flip_l in (False, True):
                    for flip_r in (False, True):
                        @pl.when((swap_l == flip_l) & (swap_r == flip_r))
                        def _():
                            if flip_l:
                                left = jnp.concatenate([units[top_l].T, units[low_l].T], axis=1)
                            else:
                                left = jnp.concatenate([units[top_l], units[low_l]], axis=0)
                            right = jnp.concatenate([units[top_r], units[low_r]], axis=0)
                            acc[...] += lax.dot_general(
                                left, right, (((1,), (1 if flip_r else 0,)), ((), ())),
                                preferred_element_type=jnp.float32,
                            )

    @pl.loop(0, 3 * block_rows)
    def _(p):
        for k in range(slots):
            done[p, k] = 0

    load.wait()

    @pl.loop(0, 2 * block_rows)
    def _(o):
        i = (o // 2) * grid_rows + r
        slot = (o % 2) * grid_cols + c
        j = l1[i, slot]
        first_product(i, j)

        @pl.when(up0 == 0)
        def _():
            at = in_list(l0, i, j)

            @pl.when(at < 2)
            def _():
                acc[...] = 2.0 * own_ref[(o // 2) * 2 + jnp.minimum(at, 1)] - acc[...]

            @pl.when(at == 2)
            def _():
                acc[...] = -acc[...]

        exact[o] = acc[...]
        cache[panel(i), slot] = acc[...].astype(jnp.bfloat16)
        done[panel(i), slot] = 1

    def ensure(i, slot):
        @pl.when(done[panel(i), slot] == 0)
        def _():
            j = l1[i, slot]
            first_product(i, j)

            @pl.when(up0 == 0)
            def _():
                at = in_list(l0, i, j)

                @pl.when(at < 2)
                def _():
                    load_oriented(i, j)
                    acc[...] = 2.0 * lhs[...].astype(jnp.float32) - acc[...]

                @pl.when(at == 2)
                def _():
                    acc[...] = -acc[...]

            cache[panel(i), slot] = acc[...].astype(jnp.bfloat16)
            done[panel(i), slot] = 1

    @pl.loop(0, 2 * block_rows)
    def _(o):
        i = (o // 2) * grid_rows + r
        j = l2[i, (o % 2) * grid_cols + c]
        out_ref[o] = jnp.zeros(out_ref.shape[1:], jnp.float32)

        @pl.loop(0, slots)
        def _(m):
            k = l1[i, m]
            at = in_list(l1, j, k)

            @pl.when(at < 2)
            def _():
                other = jnp.minimum(at, 1) * grid_cols + col_of(k)

                @pl.loop(0, 2)
                def _(side):
                    ensure(jnp.where(side == 0, i, j), jnp.where(side == 0, m, other))

                out_ref[o] += lax.dot_general(
                    cache[panel(i), m], cache[panel(j), other], (((1,), (1,)), ((), ())),
                    preferred_element_type=jnp.float32,
                )

        @pl.when(up1 == 0)
        def _():
            at = in_list(l1, i, j)

            @pl.when(at < 2)
            def _():
                out_ref[o] = 2.0 * exact[(o // 2) * 2 + jnp.minimum(at, 1)] - out_ref[o]

            @pl.when(at == 2)
            def _():
                out_ref[o] = -out_ref[o]


def replicated(pattern_in, pattern_mid, pattern_out, density):
    grid_rows = lax.axis_size("row")
    grid_cols = lax.axis_size("col")
    block_rows, _, pairs, _, edge, _ = density.shape
    mid = edge // 2
    row_slots = block_rows * pairs
    total_rows = grid_rows * block_rows
    owned = density.reshape(row_slots, edge, edge)

    units = grid_rows * grid_cols * row_slots + total_rows
    chunks = grid_cols + 1
    dma = pltpu.SemaphoreType.DMA
    smem = pl.BlockSpec(memory_space=pltpu.SMEM)
    vmem = pl.BlockSpec(memory_space=pltpu.VMEM)
    everything, total = pl.pallas_call(
        functools.partial(replicate_kernel, grid_rows, grid_cols),
        out_shape=(
            jax.ShapeDtypeStruct((units, mid, edge), jnp.bfloat16),
            jax.ShapeDtypeStruct((2, 8, 128), jnp.float32),
        ),
        in_specs=[vmem, smem],
        out_specs=(pl.BlockSpec(memory_space=pl.ANY), vmem),
        scratch_shapes=[
            pltpu.VMEM((row_slots, mid, edge), jnp.bfloat16),
            pltpu.VMEM((block_rows, mid, edge), jnp.bfloat16),
            pltpu.VMEM((4, 2, 8, 128), jnp.float32),
            pltpu.VMEM((6, 2, 8, 128), jnp.float32),
            dma((3,)),
            dma((2, chunks, 2)),
            dma((2 * chunks, 2)),
            dma((2 * chunks, 2)),
            dma((4, chunks, 2)),
            dma((grid_rows, chunks, 2)),
            dma((6,)),
            dma((6,)),
        ],
        compiler_params=pltpu.CompilerParams(
            collective_id=0, has_side_effects=True, vmem_limit_bytes=56 * 1024 * 1024
        ),
    )(owned, pattern_in)

    out = pl.pallas_call(
        functools.partial(purify_kernel, grid_rows, grid_cols),
        out_shape=jax.ShapeDtypeStruct((row_slots, edge, edge), jnp.float32),
        in_specs=[smem] * 3 + [vmem, pl.BlockSpec(memory_space=pl.ANY), vmem],
        out_specs=vmem,
        scratch_shapes=[
            pltpu.VMEM((units, mid, edge), jnp.bfloat16),
            pltpu.VMEM((edge, edge), jnp.bfloat16),
            pltpu.VMEM((edge, edge), jnp.float32),
            pltpu.VMEM((3 * block_rows, 2 * grid_cols, edge, edge), jnp.bfloat16),
            pltpu.VMEM((row_slots, edge, edge), jnp.float32),
            pltpu.SMEM((3 * block_rows, 2 * grid_cols), jnp.int32),
            pltpu.SemaphoreType.DMA,
        ],
        compiler_params=pltpu.CompilerParams(vmem_limit_bytes=56 * 1024 * 1024),
    )(pattern_in, pattern_mid, pattern_out, total, everything, owned)
    return out.reshape(density.shape)


ITERS = 2


def purify_section(owned, cur_list, next_list, grid_rows, grid_cols, row_index, col_index):
    block_rows = owned.shape[0]
    slot_pairs = owned.shape[2]
    edge_size = owned.shape[4]
    total_rows = cur_list.shape[0]
    slot_count = cur_list.shape[1]
    occupied = total_rows * edge_size / 2.0
    panels = owned.astype(jnp.bfloat16)
    owned_slots = owned[:, 0, :, 0]
    my_rows = lax.dynamic_index_in_dim(
        cur_list.reshape(block_rows, grid_rows, slot_count), row_index, axis=1, keepdims=False
    )
    my_residue = lax.dynamic_index_in_dim(
        my_rows.reshape(block_rows, slot_pairs, grid_cols), col_index, axis=2, keepdims=False
    )
    own_index = jnp.arange(block_rows, dtype=jnp.int32) * grid_rows + row_index
    diag_term = jnp.sum(
        jnp.where(my_residue == own_index[:, None], jnp.trace(owned_slots, axis1=2, axis2=3), 0.0)
    )
    next_trace = None
    trace_now = lax.psum(diag_term, ("row", "col"))
    gathered_rows = lax.all_gather(panels, "col", axis=3, tiled=True).reshape(
        block_rows, slot_count, edge_size, edge_size
    )
    next_rows = lax.dynamic_index_in_dim(
        next_list.reshape(block_rows, grid_rows, slot_count), row_index, axis=1, keepdims=False
    )
    out_cols = lax.dynamic_index_in_dim(
        next_rows.reshape(block_rows, slot_pairs, grid_cols), col_index, axis=2, keepdims=False
    )
    inner_safe = jnp.maximum(my_rows, 0)
    valid_inner = my_rows >= 0
    valid_out = out_cols >= 0
    column_panels = lax.all_gather(panels, "row", axis=1, tiled=True).reshape(
        total_rows * slot_pairs, edge_size, edge_size
    )
    residue_lists = lax.dynamic_index_in_dim(
        cur_list.reshape(total_rows, slot_pairs, grid_cols), col_index, axis=2, keepdims=False
    )
    candidates = residue_lists[inner_safe]
    matches = (
        (candidates[:, None, :, :] == out_cols[:, :, None, None])
        & valid_inner[:, None, :, None]
        & valid_out[:, :, None, None]
    )
    chosen = jnp.sum(matches * jnp.arange(slot_pairs, dtype=jnp.int32), axis=-1)
    present = jnp.any(matches, axis=-1)
    position = inner_safe[:, None, :] * slot_pairs + chosen
    picked = jnp.where(
        present[..., None, None], column_panels[position], jnp.zeros((), jnp.bfloat16)
    )
    product = jnp.einsum(
        "ikuv,ilkvw->iluw", gathered_rows, picked, preferred_element_type=jnp.float32
    )
    keep = (my_residue[:, None, :] == out_cols[:, :, None]) & valid_out[:, :, None]
    previous = jnp.sum(jnp.where(keep[..., None, None], owned_slots[:, None], 0.0), axis=2)
    updated = jnp.where(trace_now > occupied, product, 2.0 * previous - product)
    return (updated.reshape(block_rows, 1, slot_pairs, 1, edge_size, edge_size), next_trace)


def shards(pattern_in, pattern_mid, pattern_out, density_blocks):
    grid_rows = lax.axis_size("row")
    grid_cols = lax.axis_size("col")
    row_index = lax.axis_index("row")
    col_index = lax.axis_index("col")
    all_lists = (pattern_in, pattern_mid, pattern_out)
    current = density_blocks
    for iteration in range(ITERS):
        current, known_trace = purify_section(
            current,
            all_lists[iteration],
            all_lists[iteration + 1],
            grid_rows,
            grid_cols,
            row_index,
            col_index,
        )
    return current


def solution(mesh):
    in_specs = (P(), P(), P(), P(None, "row", None, "col", None, None))
    out_specs = P(None, "row", None, "col", None, None)
    plane = mesh.shape["row"] == 2 * 2 * 2 and mesh.shape["col"] == 2 * 2
    body = replicated if plane else shards
    return jax.shard_map(body, mesh=mesh, in_specs=in_specs, out_specs=out_specs, check_vma=False)
```

```python
import functools

import jax
import jax.numpy as jnp
from jax import lax
from jax.experimental import pallas as pl
from jax.experimental.pallas import tpu as pltpu
from jax.sharding import PartitionSpec as P

MESH = pl.DeviceIdType.MESH


def replicate_kernel(
    grid_rows, grid_cols, own_ref, list_ref, units_ref, total_ref,
    main_ref, extra_ref, stat_buf, stat_in,
    local_sem, send_z, send_x, send_y, send_s, recv, stat_send, stat_recv,
):
    r = lax.axis_index("row")
    z = lax.axis_index("col")
    row_slots, mid, edge = main_ref.shape
    core = r % 2
    xpos = (r // 2) % 2
    sib = r + 1 - 2 * core
    rx = r + 2 - 4 * xpos
    ry = (r + grid_rows // 2) % grid_rows
    rd = (rx + grid_rows // 2) % grid_rows
    last = grid_cols - 1
    side = z // 2
    peers = [z + 1 - 2 * (z % 2), 2 - side, last - last * side]
    pairwise = [z + 1 - 2 * (z % 2), (z + 2) % grid_cols, last - z]
    zdiag = r % grid_cols
    half = row_slots // 2
    base = grid_rows * grid_cols * row_slots
    extra_half = half // 2

    def span(row, chunk, h):
        if isinstance(chunk, str):
            return pl.ds(base + row * half + h * extra_half, extra_half)
        return pl.ds((row * grid_cols + chunk) * row_slots + h * half, half)

    def rsem(row, chunk, h):
        return recv.at[row, grid_cols if isinstance(chunk, str) else chunk, h]

    barrier = pltpu.get_barrier_semaphore()
    targets = [(sib, z), (rx, z), (ry, z)] + [(r, q) for q in peers]
    for target in targets:
        pl.semaphore_signal(barrier, inc=1, device_id=target, device_id_type=MESH)

    def pack(o):
        @pl.when(zdiag < z)
        def _():
            main_ref[o] = own_ref[o, :mid, :].astype(jnp.bfloat16)

        @pl.when(zdiag > z)
        def _():
            main_ref[o] = own_ref[o, :, mid:].astype(jnp.bfloat16).T

        @pl.when(zdiag == z)
        def _():
            top = own_ref[o, :mid, :].astype(jnp.bfloat16)
            if o % 2 == 0:
                main_ref[o] = top
                extra_ref[o // 2] = own_ref[o, mid:, :].astype(jnp.bfloat16)
            else:
                index = (o // 2) * grid_rows + r
                low = own_ref[o, :, mid:].astype(jnp.bfloat16).T
                main_ref[o] = jnp.where(index < list_ref[grid_cols + z, index], top, low)

    pending = []

    def send(src, row, chunk, h, sem, target, cond=None):
        copy = pltpu.make_async_remote_copy(
            src_ref=src,
            dst_ref=units_ref.at[span(row, chunk, h)],
            send_sem=sem,
            recv_sem=rsem(row, chunk, h),
            device_id=target,
            device_id_type=MESH,
        )
        if cond is None:
            copy.start()
        else:
            pl.when(cond)(copy.start)
        pending.append((cond, copy))

    def wait_in(row, chunk, h):
        ref = units_ref.at[span(row, chunk, h)]
        pltpu.make_async_remote_copy(
            src_ref=ref, dst_ref=ref, send_sem=local_sem.at[0], recv_sem=rsem(row, chunk, h),
            device_id=(sib, z), device_id_type=MESH,
        ).wait_recv()

    def send_col(src, chunk, origin, k, h):
        send(src, r, chunk, h, send_z.at[0, k, h], (r, (z + 1) % grid_cols), (origin <= z) & (z < last))
        send(src, r, chunk, h, send_z.at[1, k, h], (r, (z + last) % grid_cols), (origin >= z) & (z > 0))

    for h in range(2):
        for o in range(h * half, (h + 1) * half):
            pack(o)
        if h == 0:
            pl.semaphore_wait(barrier, len(targets))
        src = main_ref.at[pl.ds(h * half, half)]
        send_col(src, z, z, 0, h)
        send(src, r, z, h, send_x.at[0, h], (rx, z))
        send(src, r, z, h, send_y.at[0, h], (ry, z))
        send(src, r, z, h, send_s.at[0, 0, h], (sib, z))

    keep = pltpu.make_async_copy(
        main_ref, units_ref.at[pl.ds((r * grid_cols + z) * row_slots, row_slots)], local_sem.at[1]
    )
    keep.start()

    @pl.when(z == zdiag)
    def _():
        own = pltpu.make_async_copy(
            extra_ref, units_ref.at[pl.ds(base + r * half, half)], local_sem.at[2]
        )
        own.start()
        own.wait()

    def lanes(v):
        v = jnp.sum(v.reshape(edge // 8, 8, edge), axis=0)
        out = v[:, :128]
        for at in range(128, edge, 128):
            out = out + v[:, at:at + 128]
        return out

    stat_buf[0] = jnp.zeros(stat_buf.shape[1:], jnp.float32)
    for o in range(row_slots):
        stat_buf[0, 1] += lanes(jnp.square(own_ref[o].astype(jnp.bfloat16).astype(jnp.float32)))

    @pl.when(z == zdiag)
    def _():
        rows = lax.broadcasted_iota(jnp.int32, (edge, edge), 0)
        cols = lax.broadcasted_iota(jnp.int32, (edge, edge), 1)
        for o in range(0, row_slots, 2):
            stat_buf[0, 0] += lanes(jnp.where(rows == cols, own_ref[o], 0.0))

    plane = ((sib, z), (rx, z), (ry, z))

    def stat_copy(slot, src, target):
        return pltpu.make_async_remote_copy(
            src_ref=stat_buf.at[src], dst_ref=stat_in.at[slot], send_sem=stat_send.at[slot],
            recv_sem=stat_recv.at[slot], device_id=target, device_id_type=MESH,
        )

    def stat_step(j):
        if 0 < j <= 3:
            stat_copy(j - 1, j - 1, plane[j - 1]).wait()
            stat_buf[j] = stat_buf[j - 1] + stat_in[j - 1]
        if j < 3:
            stat_copy(j, j, plane[j]).start()
        if j == 3:
            for k in range(3):
                stat_copy(3 + k, 3, (r, pairwise[k])).start()

    def from_plane(chunk, k):
        for h in range(2):
            wait_in(rx, chunk, h)
            src = units_ref.at[span(rx, chunk, h)]
            if h == 0:
                send(src, rx, chunk, h, send_y.at[grid_cols + 1 + k, 0], (ry, z))
            send(src, rx, chunk, h, send_s.at[1, k, h], (sib, z))
            wait_in(ry, chunk, h)
            src = units_ref.at[span(ry, chunk, h)]
            if h == 1:
                send(src, ry, chunk, h, send_x.at[grid_cols + 1 + k, 0], (rx, z))
            send(src, ry, chunk, h, send_s.at[2, k, h], (sib, z))

    def from_col(chunk, k):
        for h in range(2):
            if isinstance(chunk, str):
                @pl.when(z != zdiag)
                def _():
                    wait_in(r, chunk, h)
            else:
                wait_in(r, chunk, h)
            src = units_ref.at[span(r, chunk, h)]
            send_col(src, chunk, zdiag if isinstance(chunk, str) else chunk, k, h)
            send(src, r, chunk, h, send_x.at[k, h], (rx, z))
            send(src, r, chunk, h, send_y.at[k, h], (ry, z))
            send(src, r, chunk, h, send_s.at[0, k, h], (sib, z))

    chunks = [z] + peers + ["e"]
    stat_step(0)
    for k in range(1, len(chunks)):
        from_col(chunks[k], k)
        stat_step(k)
        from_plane(chunks[k - 1], k - 1)
    from_plane(chunks[-1], len(chunks) - 1)

    for k in range(3):
        stat_copy(3 + k, 3, (r, pairwise[k])).wait()
    near = stat_buf[3] + stat_in[3]
    total_ref[...] = near + (stat_in[4] + stat_in[5])

    for k, chunk in enumerate(chunks):
        for h in range(2):
            wait_in(rd, chunk, h)
            send(units_ref.at[span(rd, chunk, h)], rd, chunk, h, send_s.at[3, k, h], (sib, z))
    for row in (sib, sib + rx - r, (sib + grid_rows // 2) % grid_rows,
                (sib + rx - r + grid_rows // 2) % grid_rows):
        for chunk in chunks:
            for h in range(2):
                wait_in(row, chunk, h)
    for cond, copy in pending:
        if cond is None:
            copy.wait_send()
        else:
            pl.when(cond)(copy.wait_send)
    keep.wait()


def purify_kernel(
    grid_rows, grid_cols, l0, l1, l2, total_ref, units, own_ref, out_ref,
    lhs, acc, cache, exact, done,
):
    r = lax.axis_index("row")
    c = lax.axis_index("col")
    block_rows = out_ref.shape[0] // 2
    total_rows = grid_rows * block_rows
    slots = 2 * grid_cols
    row_slots = 2 * block_rows
    base = grid_rows * grid_cols * row_slots
    edge = out_ref.shape[1]
    mid = edge // 2
    occupied = total_rows * edge / 2.0
    trace0 = jnp.sum(total_ref[0])
    squares = jnp.sum(total_ref[1])
    up0 = (trace0 > occupied).astype(jnp.int32)
    up1 = (jnp.where(up0 == 1, squares, 2.0 * trace0 - squares) > occupied).astype(jnp.int32)

    def col_of(i):
        return lax.rem(i, jnp.int32(grid_cols)) if grid_cols & (grid_cols - 1) else i & (grid_cols - 1)

    def row_of(i):
        return lax.rem(i, jnp.int32(grid_rows)) if grid_rows & (grid_rows - 1) else i & (grid_rows - 1)

    def by_row(i):
        return lax.div(i, jnp.int32(grid_rows)) if grid_rows & (grid_rows - 1) else i >> (grid_rows.bit_length() - 1)

    def by_col(i):
        return lax.div(i, jnp.int32(grid_cols)) if grid_cols & (grid_cols - 1) else i >> (grid_cols.bit_length() - 1)

    def panel(i):
        return jnp.where(col_of(i) == c, block_rows + by_col(i), by_row(i))

    def in_list(lists, i, j):
        cls = col_of(j)
        first = lists[cls, i] == j
        second = lists[grid_cols + cls, i] == j
        return jnp.where(first, 0, jnp.where(second, 1, 2))

    def before(i, j):
        ci, cj = col_of(i), col_of(j)
        return (ci < cj) | ((ci == cj) & (i < j))

    def unit_of(i, j):
        at = (row_of(i)) * grid_cols + col_of(j)
        return at * row_slots + (by_row(i)) * 2 + jnp.minimum(in_list(l0, i, j), 1)

    def halves(i, j):
        swap = before(j, i)
        lo = jnp.where(swap, j, i)
        hi = jnp.where(swap, i, j)
        top = unit_of(lo, hi)
        diag = base + (row_of(i)) * block_rows + by_row(i)
        low = jnp.where(i == j, diag, unit_of(hi, lo))
        return swap, top, low

    def load_oriented(i, j):
        swap, top, low = halves(i, j)

        @pl.when(swap)
        def _():
            lhs[:, :mid] = units[top].T
            lhs[:, mid:] = units[low].T

        @pl.when(jnp.logical_not(swap))
        def _():
            lhs[:mid, :] = units[top]
            lhs[mid:, :] = units[low]

    def first_product(i, j):
        acc[...] = jnp.zeros_like(acc)

        @pl.loop(0, slots)
        def _(m):
            k = l0[m, i]

            @pl.when(in_list(l0, k, j) < 2)
            def _():
                swap_l, top_l, low_l = halves(i, k)
                swap_r, top_r, low_r = halves(k, j)
                for flip_l in (False, True):
                    for flip_r in (False, True):
                        @pl.when((swap_l == flip_l) & (swap_r == flip_r))
                        def _():
                            if flip_l:
                                left = jnp.concatenate([units[top_l].T, units[low_l].T], axis=1)
                            else:
                                left = jnp.concatenate([units[top_l], units[low_l]], axis=0)
                            right = jnp.concatenate([units[top_r], units[low_r]], axis=0)
                            acc[...] += lax.dot_general(
                                left, right, (((1,), (1 if flip_r else 0,)), ((), ())),
                                preferred_element_type=jnp.float32,
                            )

    @pl.loop(0, 3 * block_rows)
    def _(p):
        for k in range(slots):
            done[p, k] = 0

    @pl.loop(0, 2 * block_rows)
    def _(o):
        i = (o // 2) * grid_rows + r
        slot = (o % 2) * grid_cols + c
        j = l1[slot, i]
        first_product(i, j)

        @pl.when(up0 == 0)
        def _():
            at = in_list(l0, i, j)

            @pl.when(at < 2)
            def _():
                acc[...] = 2.0 * own_ref[(o // 2) * 2 + jnp.minimum(at, 1)] - acc[...]

            @pl.when(at == 2)
            def _():
                acc[...] = -acc[...]

        exact[o] = acc[...]
        cache[panel(i), slot] = acc[...].astype(jnp.bfloat16)
        done[panel(i), slot] = 1

    def ensure(i, slot):
        @pl.when(done[panel(i), slot] == 0)
        def _():
            j = l1[slot, i]
            first_product(i, j)

            @pl.when(up0 == 0)
            def _():
                at = in_list(l0, i, j)

                @pl.when(at < 2)
                def _():
                    load_oriented(i, j)
                    acc[...] = 2.0 * lhs[...].astype(jnp.float32) - acc[...]

                @pl.when(at == 2)
                def _():
                    acc[...] = -acc[...]

            cache[panel(i), slot] = acc[...].astype(jnp.bfloat16)
            done[panel(i), slot] = 1

    @pl.loop(0, 2 * block_rows)
    def _(o):
        i = (o // 2) * grid_rows + r
        j = l2[(o % 2) * grid_cols + c, i]
        out_ref[o] = jnp.zeros(out_ref.shape[1:], jnp.float32)

        @pl.loop(0, slots)
        def _(m):
            k = l1[m, i]
            at = in_list(l1, j, k)

            @pl.when(at < 2)
            def _():
                other = jnp.minimum(at, 1) * grid_cols + col_of(k)

                @pl.loop(0, 2)
                def _(side):
                    ensure(jnp.where(side == 0, i, j), jnp.where(side == 0, m, other))

                out_ref[o] += lax.dot_general(
                    cache[panel(i), m], cache[panel(j), other], (((1,), (1,)), ((), ())),
                    preferred_element_type=jnp.float32,
                )

        @pl.when(up1 == 0)
        def _():
            at = in_list(l1, i, j)

            @pl.when(at < 2)
            def _():
                out_ref[o] = 2.0 * exact[(o // 2) * 2 + jnp.minimum(at, 1)] - out_ref[o]

            @pl.when(at == 2)
            def _():
                out_ref[o] = -out_ref[o]


def replicated(pattern_in, pattern_mid, pattern_out, density):
    grid_rows = lax.axis_size("row")
    grid_cols = lax.axis_size("col")
    block_rows, _, pairs, _, edge, _ = density.shape
    mid = edge // 2
    row_slots = block_rows * pairs
    total_rows = grid_rows * block_rows
    owned = density.reshape(row_slots, edge, edge)
    lists = (pattern_in.T, pattern_mid.T, pattern_out.T)

    units = grid_rows * grid_cols * row_slots + total_rows
    chunks = grid_cols + 1
    dma = pltpu.SemaphoreType.DMA
    smem = pl.BlockSpec(memory_space=pltpu.SMEM)
    vmem = pl.BlockSpec(memory_space=pltpu.VMEM)
    everything, total = pl.pallas_call(
        functools.partial(replicate_kernel, grid_rows, grid_cols),
        out_shape=(
            jax.ShapeDtypeStruct((units, mid, edge), jnp.bfloat16),
            jax.ShapeDtypeStruct((2, 8, 128), jnp.float32),
        ),
        in_specs=[vmem, smem],
        out_specs=(pl.BlockSpec(memory_space=pl.ANY), vmem),
        scratch_shapes=[
            pltpu.VMEM((row_slots, mid, edge), jnp.bfloat16),
            pltpu.VMEM((block_rows, mid, edge), jnp.bfloat16),
            pltpu.VMEM((4, 2, 8, 128), jnp.float32),
            pltpu.VMEM((6, 2, 8, 128), jnp.float32),
            dma((3,)),
            dma((2, chunks, 2)),
            dma((2 * chunks, 2)),
            dma((2 * chunks, 2)),
            dma((4, chunks, 2)),
            dma((grid_rows, chunks, 2)),
            dma((6,)),
            dma((6,)),
        ],
        compiler_params=pltpu.CompilerParams(
            collective_id=0, has_side_effects=True, vmem_limit_bytes=24 * 1024 * 1024
        ),
    )(owned, lists[0])

    out = pl.pallas_call(
        functools.partial(purify_kernel, grid_rows, grid_cols),
        out_shape=jax.ShapeDtypeStruct((row_slots, edge, edge), jnp.float32),
        in_specs=[smem] * 3 + [vmem] * 3,
        out_specs=vmem,
        scratch_shapes=[
            pltpu.VMEM((edge, edge), jnp.bfloat16),
            pltpu.VMEM((edge, edge), jnp.float32),
            pltpu.VMEM((3 * block_rows, 2 * grid_cols, edge, edge), jnp.bfloat16),
            pltpu.VMEM((row_slots, edge, edge), jnp.float32),
            pltpu.SMEM((3 * block_rows, 2 * grid_cols), jnp.int32),
        ],
        compiler_params=pltpu.CompilerParams(vmem_limit_bytes=24 * 1024 * 1024),
    )(*lists, total, everything, owned)
    return out.reshape(density.shape)


ITERS = 2


def purify_section(owned, cur_list, next_list, grid_rows, grid_cols, row_index, col_index):
    block_rows = owned.shape[0]
    slot_pairs = owned.shape[2]
    edge_size = owned.shape[4]
    total_rows = cur_list.shape[0]
    slot_count = cur_list.shape[1]
    occupied = total_rows * edge_size / 2.0
    panels = owned.astype(jnp.bfloat16)
    owned_slots = owned[:, 0, :, 0]
    my_rows = lax.dynamic_index_in_dim(
        cur_list.reshape(block_rows, grid_rows, slot_count), row_index, axis=1, keepdims=False
    )
    my_residue = lax.dynamic_index_in_dim(
        my_rows.reshape(block_rows, slot_pairs, grid_cols), col_index, axis=2, keepdims=False
    )
    own_index = jnp.arange(block_rows, dtype=jnp.int32) * grid_rows + row_index
    diag_term = jnp.sum(
        jnp.where(my_residue == own_index[:, None], jnp.trace(owned_slots, axis1=2, axis2=3), 0.0)
    )
    next_trace = None
    trace_now = lax.psum(diag_term, ("row", "col"))
    gathered_rows = lax.all_gather(panels, "col", axis=3, tiled=True).reshape(
        block_rows, slot_count, edge_size, edge_size
    )
    next_rows = lax.dynamic_index_in_dim(
        next_list.reshape(block_rows, grid_rows, slot_count), row_index, axis=1, keepdims=False
    )
    out_cols = lax.dynamic_index_in_dim(
        next_rows.reshape(block_rows, slot_pairs, grid_cols), col_index, axis=2, keepdims=False
    )
    inner_safe = jnp.maximum(my_rows, 0)
    valid_inner = my_rows >= 0
    valid_out = out_cols >= 0
    column_panels = lax.all_gather(panels, "row", axis=1, tiled=True).reshape(
        total_rows * slot_pairs, edge_size, edge_size
    )
    residue_lists = lax.dynamic_index_in_dim(
        cur_list.reshape(total_rows, slot_pairs, grid_cols), col_index, axis=2, keepdims=False
    )
    candidates = residue_lists[inner_safe]
    matches = (
        (candidates[:, None, :, :] == out_cols[:, :, None, None])
        & valid_inner[:, None, :, None]
        & valid_out[:, :, None, None]
    )
    chosen = jnp.sum(matches * jnp.arange(slot_pairs, dtype=jnp.int32), axis=-1)
    present = jnp.any(matches, axis=-1)
    position = inner_safe[:, None, :] * slot_pairs + chosen
    picked = jnp.where(
        present[..., None, None], column_panels[position], jnp.zeros((), jnp.bfloat16)
    )
    product = jnp.einsum(
        "ikuv,ilkvw->iluw", gathered_rows, picked, preferred_element_type=jnp.float32
    )
    keep = (my_residue[:, None, :] == out_cols[:, :, None]) & valid_out[:, :, None]
    previous = jnp.sum(jnp.where(keep[..., None, None], owned_slots[:, None], 0.0), axis=2)
    updated = jnp.where(trace_now > occupied, product, 2.0 * previous - product)
    return (updated.reshape(block_rows, 1, slot_pairs, 1, edge_size, edge_size), next_trace)


def shards(pattern_in, pattern_mid, pattern_out, density_blocks):
    grid_rows = lax.axis_size("row")
    grid_cols = lax.axis_size("col")
    row_index = lax.axis_index("row")
    col_index = lax.axis_index("col")
    all_lists = (pattern_in, pattern_mid, pattern_out)
    current = density_blocks
    for iteration in range(ITERS):
        current, known_trace = purify_section(
            current,
            all_lists[iteration],
            all_lists[iteration + 1],
            grid_rows,
            grid_cols,
            row_index,
            col_index,
        )
    return current


def solution(mesh):
    in_specs = (P(), P(), P(), P(None, "row", None, "col", None, None))
    out_specs = P(None, "row", None, "col", None, None)
    plane = mesh.shape["row"] == 2 * 2 * 2 and mesh.shape["col"] == 2 * 2
    body = replicated if plane else shards
    return jax.shard_map(body, mesh=mesh, in_specs=in_specs, out_specs=out_specs, check_vma=False)
```
